32 devices in a mesh: groups: 2 (over y), node: 4 (over x, core), local: 4 (over z).
Axes of the slice: x: 2, y: 2, z: 4, core: 2. Of those that a mesh axis runs over, the one named last changes fastest.
Arguments:
- tokens: bfloat16 [128, 7168], P(('groups', 'node', 'local')), parts along dimension 0, may hold values from -6 to 6
- node_list: int32 [128, 2], P(('groups', 'node', 'local')), parts along dimension 0, may hold values from 0 to 3, all different within a row; in each aligned block of 4 rows (0 to 3, 4 to 7, ...) at most 3 rows name the same one
- gates: bfloat16 [128, 4], P(('groups', 'node', 'local')), parts along dimension 0, may hold values from 0.099609375 to 1
- row_source: int32 [32, 4], P(('groups', 'node', 'local')), parts along dimension 0, may hold values from 0 to 3, each once within a row
- expert_in: bfloat16 [8, 7168, 2, 1024], P('node', None, None, 'local'), may hold values from -0.0625 to 0.0625
- expert_out: bfloat16 [8, 1024, 7168], P('node', 'local'), may hold values from -0.1875 to 0.1875
Outputs:
- mixed: bfloat16 [128, 7168], P(('groups', 'node', 'local')), parts along dimension 0
The draws below stay inside these ranges and needn't reach their ends.
There are 2 independent parts, one for each index of `groups`. The reference program is written for one: setup_inputs(seed, part) draws one part's arguments, and reference() takes and returns one part's arrays. A program takes and returns all parts, laid end to end along the dimension named above; an argument that names none is the same for every part. Nothing has to cross between parts.
Inputs may be any that keep to these rules, and one draw needn't show every extreme that they name: `node_list`: each row lists 2 different nodes. Among the 4 rows of one device no node is listed more than 3 times, and on some device some node is listed exactly 3 times. `row_source`: each row is a permutation of 0 to 3.
All inputs are finite; a program needn't handle non-finite values.
Results may differ from the reference program's by a relative error of at most 0.0095.
Values may be sent and summed in bfloat16 or wider, within the bound.
No kernel may reach another device: no remote copies, remote signals or barrier semaphores. Data moves between devices by JAX's collectives and lax.ppermute only.
A program may use at most 64 MiB of HBM per device.

```python
import math
import jax
import jax.numpy as jnp
import numpy as np
from jax import lax

D = 7168
FF = 1024
E_NODE = 2
TOK_DEV = 4
SLOTS = 2
TOPK = 4
CAP = 3
SHARES = 4
DEVS = 16
TOKENS = 64
EXPERTS = 8
N_NODE = 4


def shard_levels(rng, dims, split, low, largest):
    def one(axis_at, shards_of):
        steps = jax.random.uniform(jax.random.fold_in(jax.random.fold_in(rng, 6), axis_at), (shards_of,), jnp.float32, low / len(split), largest / len(split))
        return jnp.repeat(jnp.exp(steps), dims[axis_at] // shards_of).reshape((-1,) + (1,) * (len(dims) - axis_at - 1))

    gain = one(*split[0])
    for cut in split[1:]:
        gain = gain * one(*cut)
    return gain


def assign_block(own_key, own, number, rows, amount, top, reach, lean):
    sequence = jax.random.permutation(own_key, amount)
    crowded, ordinary = shares(amount, rows * top, reach, lean, True), shares(amount, rows * top, reach, lean, False)
    places = jnp.arange(amount)

    def named(sizes, turn):
        used = int((sizes > 0).sum())
        fixed = max(1, used // 4)
        shifted = fixed + (places - fixed + turn * (used - fixed)) % max(1, amount - fixed)
        return jnp.zeros((amount,), jnp.int32).at[sequence[jnp.where(places < fixed, places, shifted)]].set(jnp.asarray(sizes, jnp.int32))

    sizes = jnp.where(number % 4 == 0, named(crowded, number // 4), named(ordinary, number - number // 4 - 1))
    mixed = jax.random.permutation(jax.random.fold_in(own, 3), amount)
    giver, sink = mixed[0:amount // 2 * 2:2], mixed[1:amount // 2 * 2:2]
    slack = jnp.minimum(sizes[giver] - 1, reach - sizes[sink]) // 2
    slack = jnp.where((giver == sequence[0]) | (sink == sequence[0]) | (sizes[sink] == 0), 0, jnp.maximum(slack, 0))
    shifted = jax.random.randint(jax.random.fold_in(own, 4), (amount // 2,), 0, 1 << 20) % (slack + 1)
    sizes = sizes.at[giver].add(-shifted).at[sink].add(shifted)
    members = jnp.searchsorted(jnp.cumsum(sizes), jnp.arange(rows * top), side="right").astype(jnp.int32)
    grid = members.reshape(top, rows).T
    grid = grid[jax.random.permutation(jax.random.fold_in(own, 1), rows)]
    turn = jax.random.randint(jax.random.fold_in(own, 2), (rows, 1), 0, top)
    return jnp.take_along_axis(grid, (jnp.arange(top)[None, :] + turn) % top, axis=1)


def shares(amount, total, bound, slope, full):
    portions = [(1 << 20) // math.isqrt(standing ** slope) + 1 for standing in range(1, amount + 1)]
    largest = bound if full else min(bound, max(-(-total // amount), total * portions[0] // sum(portions)))
    least = 1 if total - largest >= amount - 1 else 0
    given, surplus = [largest] + [least] * (amount - 1), total - largest - least * (amount - 1)
    while surplus > 0:
        candidates = [i for i in range(1, amount) if given[i] < largest] or [i for i in range(1, amount) if given[i] < bound]
        pool, left = sum([portions[i] for i in candidates]), surplus
        for i in candidates:
            addition = min(bound - given[i], max(1, left * portions[i] // pool), surplus)
            given[i] = given[i] + addition
            surplus = surplus - addition
    return np.array(given)


def normal_values(own_key, shape, width, reach, cuts=(), kind=jnp.bfloat16):
    result = jax.random.normal(own_key, shape, jnp.float32) * width
    if len(cuts) > 0:
        result = shard_levels(own_key, shape, cuts, -0.22, 0.18) * result
    return jnp.clip(result, min=-reach, max=reach).astype(kind)


def setup_inputs(seed: int = 0, part: int = 0) -> dict:
    key_of = jax.random.split(jax.random.key(seed), 7)
    own_keys = jax.random.split(jax.random.fold_in(key_of[6], part), 7)
    tokens = normal_values(own_keys[0], (TOKENS, D), 1.0, 6.0, ((0, 16),))
    node_list_keys = jax.random.split(jax.random.fold_in(own_keys[1], 1), TOKENS // TOK_DEV)
    node_list_turns = jax.random.permutation(jax.random.fold_in(own_keys[1], 3), TOKENS // TOK_DEV)
    node_list = jax.vmap(lambda own, number: assign_block(jax.random.fold_in(own_keys[1], 2), own, number, TOK_DEV, N_NODE, SLOTS, CAP, 2))(node_list_keys, node_list_turns).reshape((TOKENS, SLOTS))
    gates = jnp.clip(jnp.exp(math.log(1.0) - 2.306499 * jax.random.uniform(own_keys[2], (TOKENS, TOPK), jnp.float32) ** shard_levels(own_keys[2], (TOKENS, TOPK), ((0, 16),), -0.2, 0.2)), 0.099609375, 1.0).astype(jnp.bfloat16)
    row_source = jax.vmap(lambda own: jax.random.permutation(own, TOK_DEV))(jax.random.split(own_keys[3], DEVS)).reshape((DEVS, TOK_DEV)).astype(jnp.int32)
    expert_in = normal_values(key_of[4], (EXPERTS, D, 2, FF), D ** -0.5, 0.0625, ((0, 4), (3, 4)))
    expert_out = normal_values(key_of[5], (EXPERTS, FF, D), FF ** -0.5, 0.1875, ((0, 4), (1, 4)))
    return {"tokens": tokens, "node_list": node_list, "gates": gates, "row_source": row_source, "expert_in": expert_in, "expert_out": expert_out}


def reference(tokens, node_list, gates, row_source, expert_in, expert_out):
    flat_node = node_list.reshape(TOKENS * SLOTS)
    flat_gate = gates.reshape(TOKENS * SLOTS, E_NODE)
    limit = DEVS * CAP
    share_units = FF // SHARES

    def one_node(node):
        marks = jnp.where(flat_node == node, 0, 1).astype(jnp.int32)
        order = jnp.argsort(marks, stable=True)[:limit].astype(jnp.int32)
        valid = flat_node[order] == node
        owner = (order // SLOTS).astype(jnp.int32)
        rows = tokens[owner].astype(jnp.float32)
        start = (node * E_NODE).astype(jnp.int32)
        weight_in = lax.dynamic_slice_in_dim(expert_in, start, E_NODE, 0).astype(jnp.float32)
        weight_out = lax.dynamic_slice_in_dim(expert_out, start, E_NODE, 0).astype(jnp.float32)
        proj = jnp.einsum("rd,edgf->regf", rows, weight_in)
        pairs = jnp.where(valid[:, None], flat_gate[order].astype(jnp.float32), jnp.float32(0.0))
        hidden = (jax.nn.silu(proj[:, :, 0]) * proj[:, :, 1] * pairs[:, :, None]).astype(jnp.bfloat16)
        hidden_split = hidden.astype(jnp.float32).reshape(limit, E_NODE, SHARES, share_units)
        weight_split = weight_out.reshape(E_NODE, SHARES, share_units, D)
        part_out = jnp.einsum("resf,esfd->srd", hidden_split, weight_split).astype(jnp.bfloat16)
        part_out = lax.optimization_barrier(part_out)
        output = jnp.sum(part_out.astype(jnp.float32), axis=0).astype(jnp.bfloat16)
        return owner, output

    owners, outputs = lax.map(one_node, jnp.arange(N_NODE, dtype=jnp.int32))
    total = jnp.zeros((TOKENS, D), jnp.float32).at[owners.reshape(-1)].add(outputs.reshape(-1, D).astype(jnp.float32))
    combined = total.astype(jnp.bfloat16).reshape(DEVS, TOK_DEV, D)
    mixed = jnp.take_along_axis(combined, row_source.astype(jnp.int32)[:, :, None], axis=1)
    return mixed.reshape(TOKENS, D)
```

```python
import jax
import jax.numpy as jnp
from jax import lax
from jax.sharding import PartitionSpec as P

AXES = ("node", "local")


def swap(value, mask, count):
    return lax.ppermute(value, AXES, [(i, i ^ mask) for i in range(count)])


def shards(tokens, node_list, gates, row_source, expert_in, expert_out):
    rows, width = tokens.shape
    slots = node_list.shape[1]
    pair = expert_in.shape[0]
    units = expert_in.shape[3]
    nodes = lax.axis_size("node")
    locals_ = lax.axis_size("local")
    count = nodes * locals_
    hit = (node_list[:, :, None] == jnp.arange(nodes, dtype=jnp.int32)).astype(jnp.float32)
    dense = jnp.sum(
        hit[:, :, :, None] * gates.reshape(rows, slots, 1, pair).astype(jnp.float32), axis=1
    ).reshape(rows, nodes * pair)
    extra = -(-nodes * pair // 128) * 128
    message = jnp.concatenate(
        [tokens, jnp.pad(dense, ((0, 0), (0, extra - nodes * pair))).astype(jnp.bfloat16)], axis=1
    )
    pick = (row_source.reshape(rows)[:, None] == jnp.arange(rows, dtype=jnp.int32)).astype(
        jnp.bfloat16
    )
    message = jnp.dot(pick, message, preferred_element_type=jnp.float32).astype(jnp.bfloat16)
    along = jnp.concatenate(
        [message] + [swap(message, k, count) for k in range(1, locals_)], axis=0
    )
    across = jnp.concatenate(
        [along] + [swap(along, k * 2 * locals_, count) for k in range(1, nodes // 2)], axis=0
    )
    everything = jnp.concatenate([across, swap(across, locals_, count)], axis=0)
    total = everything.shape[0]
    mine = (jnp.arange(nodes) == lax.axis_index("node")).astype(jnp.float32)
    weight = jnp.sum(
        everything[:, width : width + nodes * pair].astype(jnp.float32).reshape(total, nodes, pair)
        * mine[None, :, None],
        axis=1,
    )
    proj = jnp.einsum(
        "rd,edgf->regf", everything[:, :width], expert_in, preferred_element_type=jnp.float32
    )
    hidden = (
        (jax.nn.silu(proj[:, :, 0]) * proj[:, :, 1] * weight[:, :, None])
        .astype(jnp.bfloat16)
        .reshape(total, pair * units)
    )
    out = jnp.dot(
        hidden, expert_out.reshape(pair * units, width), preferred_element_type=jnp.float32
    ).astype(jnp.bfloat16)
    half = total // 2
    out = (
        out[:half].astype(jnp.float32) + swap(out[half:], locals_, count).astype(jnp.float32)
    ).astype(jnp.bfloat16)
    step = rows * locals_
    parts = [out[:step]] + [
        swap(out[k * step : (k + 1) * step], k * 2 * locals_, count) for k in range(1, nodes // 2)
    ]
    out = sum(p.astype(jnp.float32) for p in parts).astype(jnp.bfloat16)
    parts = [out[:rows]] + [
        swap(out[k * rows : (k + 1) * rows], k, count) for k in range(1, locals_)
    ]
    return sum(p.astype(jnp.float32) for p in parts).astype(jnp.bfloat16)


def solution(mesh):
    spec = P(("groups", "node", "local"), None)
    return jax.shard_map(
        shards,
        mesh=mesh,
        in_specs=(spec, spec, spec, spec, P("node", None, None, "local"), P("node", "local", None)),
        out_specs=spec,
        check_vma=False,
    )
```

```python
import functools

import jax
import jax.numpy as jnp
from jax import lax
from jax.experimental import pallas as pl
from jax.experimental.pallas import tpu as pltpu
from jax.sharding import PartitionSpec as P

AXES = ("node", "local")
VMEM = pltpu.VMEM
LANES = 128
BUFFERS = 3


def swap(value, mask, count):
    return lax.ppermute(value, AXES, [(i, i ^ mask) for i in range(count)])


def in_vmem(count):
    return [pl.BlockSpec(memory_space=VMEM)] * count


def pack_kernel(tokens, gates, nodes, out):
    rows, width = tokens.shape
    chosen = gates.shape[1]
    slots = nodes.shape[0]
    out[:, :width] = tokens[...]
    tail = jnp.concatenate(
        [gates[...].astype(jnp.float32), jnp.zeros((rows, LANES - chosen), jnp.float32)], axis=1
    )
    row = lax.broadcasted_iota(jnp.int32, (rows, LANES), 0)
    lane = lax.broadcasted_iota(jnp.int32, (rows, LANES), 1)
    for r in range(rows):
        for j in range(slots):
            tail = jnp.where(
                (row == r) & (lane == chosen + j), nodes[j, r].astype(jnp.float32), tail
            )
    out[:, width:] = tail.astype(jnp.bfloat16)


def pack(tokens, gates, node_list):
    rows, width = tokens.shape
    return pl.pallas_call(
        pack_kernel,
        out_shape=jax.ShapeDtypeStruct((rows, width + LANES), jnp.bfloat16),
        in_specs=in_vmem(2) + [pl.BlockSpec(memory_space=pltpu.SMEM)],
        out_specs=pl.BlockSpec(memory_space=VMEM),
    )(tokens, gates, node_list.T)


def sort_kernel(chunk, kinds, source, out, buffer, wide, sem):
    pair, total, _ = source.shape
    steps = total // chunk
    depth = chunk // kinds
    count = pair * steps

    def fetch(i, slot):
        start = pl.multiple_of(lax.rem(i, steps) * chunk, chunk)
        return pltpu.make_async_copy(
            source.at[i // steps, pl.ds(start, chunk)], buffer.at[slot], sem.at[slot]
        )

    for i in range(BUFFERS - 1):
        fetch(i, i).start()

    @pl.loop(0, count)
    def _(i):
        slot = lax.rem(i, BUFFERS)

        @pl.when(i + BUFFERS - 1 < count)
        def _():
            fetch(i + BUFFERS - 1, lax.rem(i + BUFFERS - 1, BUFFERS)).start()

        fetch(i, slot).wait()
        wide[...] = buffer[slot].astype(jnp.float32)
        at = pl.multiple_of(lax.rem(i, steps) * depth, depth)
        for k in range(kinds):
            column = (k % 2) * (kinds // 2) + k // 2
            out[i // steps, pl.ds(at, depth), column * LANES : (column + 1) * LANES] = wide[
                pl.ds(k, depth, stride=kinds), :
            ].astype(jnp.bfloat16)


def sort_weights(weight):
    pair, depth, two, units = weight.shape
    blocks = units // LANES
    kinds = two * blocks
    view = (
        weight.reshape(pair, depth, two, blocks, LANES)
        .transpose(0, 1, 3, 2, 4)
        .reshape(pair, depth * kinds, LANES)
    )
    chunk = 1024 * kinds
    return pl.pallas_call(
        functools.partial(sort_kernel, chunk, kinds),
        out_shape=VMEM((pair, depth, two * units), jnp.bfloat16),
        in_specs=[pl.BlockSpec(memory_space=pl.ANY)],
        out_specs=pl.BlockSpec(memory_space=VMEM),
        scratch_shapes=[
            VMEM((BUFFERS, chunk, LANES), jnp.bfloat16),
            VMEM((chunk, LANES), jnp.float32),
            pltpu.SemaphoreType.DMA((BUFFERS,)),
        ],
        compiler_params=pltpu.CompilerParams(vmem_limit_bytes=12 << 20),
        cost_estimate=pl.CostEstimate(flops=0, bytes_accessed=weight.size * 4, transcendentals=0),
    )(view)


def expert_kernel(chosen, near, far, weight_in, weight_out, out, held, hidden):
    half = near.shape[0]
    pair, depth, columns = weight_in.shape
    units = columns // 2
    slots = chosen // pair
    held[:half] = near[...]
    held[half:] = far[...]
    rows = held[:, :depth]
    tail = held[:, depth:].astype(jnp.float32)
    node = lax.axis_index("node").astype(jnp.float32)
    for e in range(pair):
        gate = jnp.zeros((2 * half, 1), jnp.float32)
        for j in range(slots):
            listed = tail[:, chosen + j : chosen + j + 1] == node
            gate = gate + jnp.where(listed, tail[:, pair * j + e : pair * j + e + 1], 0.0)
        first = jnp.dot(rows, weight_in[e, :, :units], preferred_element_type=jnp.float32)
        second = jnp.dot(rows, weight_in[e, :, units:], preferred_element_type=jnp.float32)
        active = first / (1.0 + jnp.exp(-first)) * second * gate
        hidden[:, e * units : (e + 1) * units] = active.astype(jnp.bfloat16)
    tile = 512

    @pl.loop(0, depth // tile)
    def _(i):
        at = pl.multiple_of(i * tile, tile)
        out[:, pl.ds(at, tile)] = jnp.dot(
            hidden[...], weight_out[:, pl.ds(at, tile)], preferred_element_type=jnp.float32
        ).astype(jnp.bfloat16)


def experts(chosen, near, far, weight_in, weight_out):
    half = near.shape[0]
    pair, depth, columns = weight_in.shape
    weight_out = weight_out.reshape(-1, depth)
    held = [pltpu.with_memory_space_constraint(a, VMEM) for a in (near, far, weight_in, weight_out)]
    return pl.pallas_call(
        functools.partial(expert_kernel, chosen),
        out_shape=VMEM((2 * half, depth), jnp.bfloat16),
        in_specs=in_vmem(4),
        out_specs=pl.BlockSpec(memory_space=VMEM),
        scratch_shapes=[
            VMEM((2 * half, near.shape[1]), jnp.bfloat16),
            VMEM((2 * half, weight_out.shape[0]), jnp.bfloat16),
        ],
        compiler_params=pltpu.CompilerParams(vmem_limit_bytes=16 << 20),
        cost_estimate=pl.CostEstimate(
            flops=6 * half * weight_in.size, bytes_accessed=1 << 20, transcendentals=0
        ),
    )(*held)


def finish_kernel(count, source, *refs):
    out = refs[count]
    total = sum(r[...].astype(jnp.float32) for r in refs[:count])
    rows = total.shape[0]
    picked = []
    for r in range(rows):
        line = total[0:1]
        for k in range(1, rows):
            line = jnp.where(source[0, r] == k, total[k : k + 1], line)
        picked.append(line)
    out[...] = jnp.concatenate(picked, axis=0).astype(jnp.bfloat16)


def finish(row_source, parts):
    return pl.pallas_call(
        functools.partial(finish_kernel, len(parts)),
        out_shape=jax.ShapeDtypeStruct(parts[0].shape, jnp.bfloat16),
        in_specs=[pl.BlockSpec(memory_space=pltpu.SMEM)] + in_vmem(len(parts)),
        out_specs=pl.BlockSpec(memory_space=VMEM),
    )(row_source, *parts)


def shards(tokens, node_list, gates, row_source, expert_in, expert_out):
    rows, width = tokens.shape
    nodes = lax.axis_size("node")
    locals_ = lax.axis_size("local")
    count = nodes * locals_
    weight_in = sort_weights(expert_in)
    message = pack(tokens, gates, node_list)
    along = jnp.concatenate(
        [message] + [swap(message, k, count) for k in range(1, locals_)], axis=0
    )
    across = jnp.concatenate(
        [along] + [swap(along, k * 2 * locals_, count) for k in range(1, nodes // 2)], axis=0
    )
    out = experts(gates.shape[1], across, swap(across, locals_, count), weight_in, expert_out)
    half = across.shape[0]
    out = (
        out[:half].astype(jnp.float32) + swap(out[half:], locals_, count).astype(jnp.float32)
    ).astype(jnp.bfloat16)
    step = rows * locals_
    parts = [out[:step]] + [
        swap(out[k * step : (k + 1) * step], k * 2 * locals_, count) for k in range(1, nodes // 2)
    ]
    out = sum(p.astype(jnp.float32) for p in parts).astype(jnp.bfloat16)
    parts = [out[:rows]] + [
        swap(out[k * rows : (k + 1) * rows], k, count) for k in range(1, locals_)
    ]
    return finish(row_source, parts)


def solution(mesh):
    spec = P(("groups", "node", "local"), None)
    return jax.shard_map(
        shards,
        mesh=mesh,
        in_specs=(spec, spec, spec, spec, P("node", None, None, "local"), P("node", "local", None)),
        out_specs=spec,
        check_vma=False,
    )
```

```python
import functools

import jax
import jax.numpy as jnp
from jax import lax
from jax.experimental import pallas as pl
from jax.experimental.pallas import tpu as pltpu
from jax.sharding import PartitionSpec as P

AXES = ("node", "local")
VMEM = pltpu.VMEM
LANES = 128
BUFFERS = 8
PIECE = 1024
SMALL = pltpu.CompilerParams(vmem_limit_bytes=4 << 20)


def swap(value, mask, count):
    return lax.ppermute(value, AXES, [(i, i ^ mask) for i in range(count)])


def in_vmem(count):
    return [pl.BlockSpec(memory_space=VMEM)] * count


def hold(*arrays):
    return [pltpu.with_memory_space_constraint(a, VMEM) for a in arrays]


def local_call(kernel, shapes, operands):
    return pl.pallas_call(
        kernel,
        out_shape=tuple(VMEM(s, jnp.bfloat16) for s in shapes),
        in_specs=in_vmem(len(operands)),
        out_specs=tuple(in_vmem(len(shapes))),
        compiler_params=SMALL,
    )(*hold(*operands))


def pack_kernel(tokens, gates, nodes, source, out):
    rows, width = tokens.shape
    chosen = gates.shape[1]
    slots = nodes.shape[0]
    out[:, :width] = tokens[...]
    tail = jnp.concatenate(
        [gates[...].astype(jnp.float32), jnp.zeros((rows, LANES - chosen), jnp.float32)], axis=1
    )
    row = lax.broadcasted_iota(jnp.int32, (rows, LANES), 0)
    lane = lax.broadcasted_iota(jnp.int32, (rows, LANES), 1)
    for r in range(rows):
        numbers = [nodes[j, r] for j in range(slots)] + [source[0, r]]
        for j, number in enumerate(numbers):
            tail = jnp.where((row == r) & (lane == chosen + j), number.astype(jnp.float32), tail)
    out[:, width:] = tail.astype(jnp.bfloat16)


def pack(tokens, gates, node_list, row_source):
    rows, width = tokens.shape
    return pl.pallas_call(
        pack_kernel,
        out_shape=VMEM((rows, width + LANES), jnp.bfloat16),
        in_specs=in_vmem(2) + [pl.BlockSpec(memory_space=pltpu.SMEM)] * 2,
        out_specs=pl.BlockSpec(memory_space=VMEM),
    )(tokens, gates, node_list.T, row_source)


def sort_kernel(chunk, kinds, expert, source, out, token, buffer, wide, sem):
    _, total, _ = source.shape
    count = total // chunk
    depth = chunk // kinds

    def fetch(i, slot):
        start = pl.multiple_of(i * chunk, chunk)
        return pltpu.make_async_copy(
            source.at[expert, pl.ds(start, chunk)], buffer.at[slot], sem.at[slot]
        )

    for i in range(BUFFERS - 1):
        fetch(i, i).start()

    @pl.loop(0, count)
    def _(i):
        slot = lax.rem(i, BUFFERS)

        @pl.when(i + BUFFERS - 1 < count)
        def _():
            fetch(i + BUFFERS - 1, lax.rem(i + BUFFERS - 1, BUFFERS)).start()

        fetch(i, slot).wait()
        wide[...] = buffer[slot].astype(jnp.float32)
        at = pl.multiple_of(i * depth, depth)
        for k in range(kinds):
            column = (k % 2) * (kinds // 2) + k // 2
            out[pl.ds(at, depth), column * LANES : (column + 1) * LANES] = wide[
                pl.ds(k, depth, stride=kinds), :
            ].astype(jnp.bfloat16)

    token[...] = jnp.zeros_like(token)


def sort_weights(weight):
    pair, depth, two, units = weight.shape
    blocks = units // LANES
    kinds = two * blocks
    view = (
        weight.reshape(pair, depth, two, blocks, LANES)
        .transpose(0, 1, 3, 2, 4)
        .reshape(pair, depth * kinds, LANES)
    )
    chunk = 512 * kinds
    return [
        pl.pallas_call(
            functools.partial(sort_kernel, chunk, kinds, expert),
            out_shape=(VMEM((depth, two * units), jnp.bfloat16), VMEM((16, LANES), jnp.bfloat16)),
            in_specs=[pl.BlockSpec(memory_space=pltpu.HBM)],
            out_specs=tuple(in_vmem(2)),
            scratch_shapes=[
                VMEM((BUFFERS, chunk, LANES), jnp.bfloat16),
                VMEM((chunk, LANES), jnp.float32),
                pltpu.SemaphoreType.DMA((BUFFERS,)),
            ],
            compiler_params=pltpu.CompilerParams(vmem_limit_bytes=8 << 20),
            cost_estimate=pl.CostEstimate(
                flops=0, bytes_accessed=2 * weight.size, transcendentals=0
            ),
        )(pltpu.with_memory_space_constraint(view, pltpu.HBM))
        for expert in range(pair)
    ]


def expert_kernel(chosen, pair, rows, near, far, *refs):
    weight_in, weight_out = refs[:pair], refs[pair]
    near_out, far_out, held, hidden, down, sem = refs[pair + 1 :]
    half = near.shape[0]
    depth, columns = weight_in[0].shape
    units = columns // 2
    slots = chosen // pair
    total = 2 * half
    pieces = range(0, depth, PIECE)
    copies = [
        pltpu.make_async_copy(
            weight_out.at[:, pl.ds(at, PIECE)], down.at[:, pl.ds(at, PIECE)], sem.at[i]
        )
        for i, at in enumerate(pieces)
    ]
    for copy in copies:
        copy.start()
    held[:half] = near[...]
    held[half:] = far[...]
    tail = held[:, depth:].astype(jnp.float32)
    node = lax.axis_index("node").astype(jnp.float32)
    active = []
    for e in range(pair):
        gate = jnp.zeros((total, 1), jnp.float32)
        for j in range(slots):
            listed = tail[:, chosen + j : chosen + j + 1] == node
            gate = gate + jnp.where(listed, tail[:, pair * j + e : pair * j + e + 1], 0.0)
        first = jnp.dot(held[:, :depth], weight_in[e][:, :units], preferred_element_type=jnp.float32)
        second = jnp.dot(
            held[:, :depth], weight_in[e][:, units:], preferred_element_type=jnp.float32
        )
        active.append((first / (1.0 + jnp.exp(-first)) * second * gate).astype(jnp.bfloat16))
    row = lax.broadcasted_iota(jnp.int32, (total, total), 0)
    column = lax.broadcasted_iota(jnp.int32, (total, total), 1)
    source = tail[:, chosen + slots : chosen + slots + 1].astype(jnp.int32)
    order = (column == row - lax.rem(row, rows) + source).astype(jnp.bfloat16)
    hidden[...] = jnp.dot(
        order, jnp.concatenate(active, axis=1), preferred_element_type=jnp.float32
    ).astype(jnp.bfloat16)
    for copy, at in zip(copies, pieces):
        copy.wait()
        result = jnp.dot(
            hidden[...], down[:, at : at + PIECE], preferred_element_type=jnp.float32
        ).astype(jnp.bfloat16)
        near_out[:, at : at + PIECE] = result[:half]
        far_out[:, at : at + PIECE] = result[half:]


def experts(chosen, rows, near, far, weight_in, weight_out):
    half = near.shape[0]
    pair = len(weight_in)
    depth, columns = weight_in[0].shape
    weight_out = pltpu.with_memory_space_constraint(weight_out.reshape(-1, depth), pltpu.HBM)
    return pl.pallas_call(
        functools.partial(expert_kernel, chosen, pair, rows),
        out_shape=(VMEM((half, depth), jnp.bfloat16),) * 2,
        in_specs=in_vmem(2 + pair) + [pl.BlockSpec(memory_space=pltpu.HBM)],
        out_specs=tuple(in_vmem(2)),
        scratch_shapes=[
            VMEM((2 * half, near.shape[1]), jnp.bfloat16),
            VMEM((2 * half, weight_out.shape[0]), jnp.bfloat16),
            VMEM(weight_out.shape, jnp.bfloat16),
            pltpu.SemaphoreType.DMA((depth // PIECE,)),
        ],
        compiler_params=pltpu.CompilerParams(vmem_limit_bytes=24 << 20),
        cost_estimate=pl.CostEstimate(
            flops=6 * half * pair * weight_in[0].size, bytes_accessed=8 << 20, transcendentals=0
        ),
    )(*hold(near, far, *weight_in), weight_out)


def join(operands, *after):
    count = len(operands)

    def kernel(*refs):
        refs[-1][...] = jnp.concatenate([r[...] for r in refs[:count]], axis=0)

    shape = (sum(a.shape[0] for a in operands), operands[0].shape[1])
    return local_call(kernel, [shape], [*operands, *after])[0]


def fold_kernel(near, far, *outs):
    total = near[...].astype(jnp.float32) + far[...].astype(jnp.float32)
    at = 0
    for out in outs:
        out[...] = total[at : at + out.shape[0]].astype(jnp.bfloat16)
        at += out.shape[0]


def split_kernel(count, rows, head, head_got, *refs):
    top = head[...].astype(jnp.float32) + head_got[...].astype(jnp.float32)
    low = sum(r[...].astype(jnp.float32) for r in refs[:count])
    both = jnp.concatenate([top, low], axis=0)
    for i, out in enumerate(refs[count:]):
        out[...] = both[i * rows : (i + 1) * rows].astype(jnp.bfloat16)


def shards(tokens, node_list, gates, row_source, expert_in, expert_out):
    rows, width = tokens.shape
    nodes = lax.axis_size("node")
    locals_ = lax.axis_size("local")
    count = nodes * locals_
    step = 2 * locals_
    across = range(1, nodes // 2)
    beyond = range(2, locals_)
    message = pack(tokens, gates, node_list, row_source)
    (first, first_done), *later = sort_weights(expert_in)
    tail = [swap(message, k, count) for k in beyond]
    head = [message] + [swap(message, a * step, count) for a in across]
    head, tail = join(head, first_done), join(tail, first_done)
    near = [head, tail, swap(head, 1, count)] + [swap(tail, a * step, count) for a in across]
    near = join(near, *[done for _, done in later])
    near_out, far_out = experts(
        gates.shape[1],
        rows,
        near,
        swap(near, locals_, count),
        [first] + [w for w, _ in later],
        expert_out,
    )
    sizes = [head.shape[0], tail.shape[0], head.shape[0]] + [tail.shape[0]] * len(across)
    head, tail, side, *sides = local_call(
        fold_kernel, [(s, width) for s in sizes], [near_out, swap(far_out, locals_, count)]
    )
    head_got = swap(side, 1, count)
    tail_got = [swap(v, a * step, count) for a, v in zip(across, sides)]
    own, *others = local_call(
        functools.partial(split_kernel, 1 + len(across), rows),
        [(rows, width)] * (1 + len(across) + len(beyond)),
        [head, head_got, tail, *tail_got],
    )
    masks = [a * step for a in across] + list(beyond)
    got = [swap(v, m, count) for m, v in reversed(list(zip(masks, others)))]
    return sum(v.astype(jnp.float32) for v in [own, *got]).astype(jnp.bfloat16)


def solution(mesh):
    spec = P(("groups", "node", "local"), None)
    return jax.shard_map(
        shards,
        mesh=mesh,
        in_specs=(spec, spec, spec, spec, P("node", None, None, "local"), P("node", "local", None)),
        out_specs=spec,
        check_vma=False,
    )
```

```python
import functools

import jax
import jax.numpy as jnp
from jax import lax
from jax.experimental import pallas as pl
from jax.experimental.pallas import tpu as pltpu
from jax.sharding import PartitionSpec as P

AXES = ("node", "local")
VMEM = pltpu.VMEM
LANES = 128
BUFFERS = 8
PIECE = 1024
EARLY = (2, 2)
SMALL = pltpu.CompilerParams(vmem_limit_bytes=4 << 20)


def swap(value, mask, count):
    return lax.ppermute(value, AXES, [(i, i ^ mask) for i in range(count)])


def in_vmem(count):
    return [pl.BlockSpec(memory_space=VMEM)] * count


def hold(*arrays):
    return [pltpu.with_memory_space_constraint(a, VMEM) for a in arrays]


def local_call(kernel, shapes, operands):
    return pl.pallas_call(
        kernel,
        out_shape=tuple(VMEM(s, jnp.bfloat16) for s in shapes),
        in_specs=in_vmem(len(operands)),
        out_specs=tuple(in_vmem(len(shapes))),
        compiler_params=SMALL,
    )(*hold(*operands))


def pack_kernel(tokens, gates, nodes, source, out):
    rows, width = tokens.shape
    chosen = gates.shape[1]
    slots = nodes.shape[0]
    out[:, :width] = tokens[...]
    tail = jnp.concatenate(
        [gates[...].astype(jnp.float32), jnp.zeros((rows, LANES - chosen), jnp.float32)], axis=1
    )
    row = lax.broadcasted_iota(jnp.int32, (rows, LANES), 0)
    lane = lax.broadcasted_iota(jnp.int32, (rows, LANES), 1)
    for r in range(rows):
        numbers = [nodes[j, r] for j in range(slots)] + [source[0, r]]
        for j, number in enumerate(numbers):
            tail = jnp.where((row == r) & (lane == chosen + j), number.astype(jnp.float32), tail)
    out[:, width:] = tail.astype(jnp.bfloat16)


def pack(tokens, gates, node_list, row_source):
    rows, width = tokens.shape
    return pl.pallas_call(
        pack_kernel,
        out_shape=VMEM((rows, width + LANES), jnp.bfloat16),
        in_specs=in_vmem(2) + [pl.BlockSpec(memory_space=pltpu.SMEM)] * 2,
        out_specs=pl.BlockSpec(memory_space=VMEM),
    )(tokens, gates, node_list.T, row_source)


def sort_kernel(chunk, kinds, expert, start_at, source, down, out, part, buffer, wide, sem, down_sem):
    _, total, _ = source.shape
    count = total // chunk
    depth = chunk // kinds

    def fetch(i, slot):
        start = pl.multiple_of(i * chunk, chunk)
        return pltpu.make_async_copy(
            source.at[expert, pl.ds(start, chunk)], buffer.at[slot], sem.at[slot]
        )

    for i in range(BUFFERS - 1):
        fetch(i, i).start()
    extra = pltpu.make_async_copy(down.at[:, pl.ds(start_at, part.shape[1])], part, down_sem)
    extra.start()

    @pl.loop(0, count)
    def _(i):
        slot = lax.rem(i, BUFFERS)

        @pl.when(i + BUFFERS - 1 < count)
        def _():
            fetch(i + BUFFERS - 1, lax.rem(i + BUFFERS - 1, BUFFERS)).start()

        fetch(i, slot).wait()
        wide[...] = buffer[slot].astype(jnp.float32)
        at = pl.multiple_of(i * depth, depth)
        for k in range(kinds):
            column = (k % 2) * (kinds // 2) + k // 2
            out[pl.ds(at, depth), column * LANES : (column + 1) * LANES] = wide[
                pl.ds(k, depth, stride=kinds), :
            ].astype(jnp.bfloat16)

    extra.wait()


def sort_weights(weight, down):
    pair, depth, two, units = weight.shape
    blocks = units // LANES
    kinds = two * blocks
    view = (
        weight.reshape(pair, depth, two, blocks, LANES)
        .transpose(0, 1, 3, 2, 4)
        .reshape(pair, depth * kinds, LANES)
    )
    chunk = 512 * kinds
    down = down.reshape(-1, depth)
    ends = [sum(EARLY[:e]) * PIECE for e in range(pair + 1)]
    source = [pltpu.with_memory_space_constraint(a, pltpu.HBM) for a in (view, down)]
    return [
        pl.pallas_call(
            functools.partial(sort_kernel, chunk, kinds, expert, ends[expert]),
            out_shape=(
                VMEM((depth, two * units), jnp.bfloat16),
                VMEM((down.shape[0], ends[expert + 1] - ends[expert]), jnp.bfloat16),
            ),
            in_specs=[pl.BlockSpec(memory_space=pltpu.HBM)] * 2,
            out_specs=tuple(in_vmem(2)),
            scratch_shapes=[
                VMEM((BUFFERS, chunk, LANES), jnp.bfloat16),
                VMEM((chunk, LANES), jnp.float32),
                pltpu.SemaphoreType.DMA((BUFFERS,)),
                pltpu.SemaphoreType.DMA,
            ],
            compiler_params=pltpu.CompilerParams(vmem_limit_bytes=8 << 20),
            cost_estimate=pl.CostEstimate(
                flops=0, bytes_accessed=2 * weight.size, transcendentals=0
            ),
        )(*source)
        for expert in range(pair)
    ]


def expert_kernel(chosen, pair, rows, near, far, *refs):
    weight_in, weight_out = refs[:pair], refs[pair:-4]
    near_out, far_out, held, hidden = refs[-4:]
    half = near.shape[0]
    depth, columns = weight_in[0].shape
    units = columns // 2
    slots = chosen // pair
    total = 2 * half
    held[:half] = near[...]
    held[half:] = far[...]
    tail = held[:, depth:].astype(jnp.float32)
    node = lax.axis_index("node").astype(jnp.float32)
    active = []
    for e in range(pair):
        gate = jnp.zeros((total, 1), jnp.float32)
        for j in range(slots):
            listed = tail[:, chosen + j : chosen + j + 1] == node
            gate = gate + jnp.where(listed, tail[:, pair * j + e : pair * j + e + 1], 0.0)
        first = jnp.dot(held[:, :depth], weight_in[e][:, :units], preferred_element_type=jnp.float32)
        second = jnp.dot(
            held[:, :depth], weight_in[e][:, units:], preferred_element_type=jnp.float32
        )
        active.append((first / (1.0 + jnp.exp(-first)) * second * gate).astype(jnp.bfloat16))
    row = lax.broadcasted_iota(jnp.int32, (total, total), 0)
    column = lax.broadcasted_iota(jnp.int32, (total, total), 1)
    source = tail[:, chosen + slots : chosen + slots + 1].astype(jnp.int32)
    order = (column == row - lax.rem(row, rows) + source).astype(jnp.bfloat16)
    hidden[...] = jnp.dot(
        order, jnp.concatenate(active, axis=1), preferred_element_type=jnp.float32
    ).astype(jnp.bfloat16)
    at = 0
    for down in weight_out:
        for i in range(down.shape[1] // PIECE):
            result = jnp.dot(
                hidden[...],
                down[:, i * PIECE : (i + 1) * PIECE],
                preferred_element_type=jnp.float32,
            ).astype(jnp.bfloat16)
            near_out[:, at : at + PIECE] = result[:half]
            far_out[:, at : at + PIECE] = result[half:]
            at += PIECE


def load_kernel(begin, source, after, out, sem):
    copy = pltpu.make_async_copy(source.at[:, pl.ds(begin, out.shape[1])], out, sem)
    copy.start()
    copy.wait()


def load(weight_out, begin, after):
    weight_out = pltpu.with_memory_space_constraint(
        weight_out.reshape(-1, weight_out.shape[-1]), pltpu.HBM
    )
    height, depth = weight_out.shape
    return pl.pallas_call(
        functools.partial(load_kernel, begin),
        out_shape=VMEM((height, depth - begin), jnp.bfloat16),
        in_specs=[pl.BlockSpec(memory_space=pltpu.HBM)] + in_vmem(1),
        out_specs=pl.BlockSpec(memory_space=VMEM),
        scratch_shapes=[pltpu.SemaphoreType.DMA],
        compiler_params=SMALL,
        cost_estimate=pl.CostEstimate(
            flops=0, bytes_accessed=2 * height * (depth - begin), transcendentals=0
        ),
    )(weight_out, *hold(after))


def experts(chosen, rows, near, far, weight_in, weight_out):
    half = near.shape[0]
    pair = len(weight_in)
    depth, columns = weight_in[0].shape
    return pl.pallas_call(
        functools.partial(expert_kernel, chosen, pair, rows),
        out_shape=(VMEM((half, depth), jnp.bfloat16),) * 2,
        in_specs=in_vmem(2 + pair + len(weight_out)),
        out_specs=tuple(in_vmem(2)),
        scratch_shapes=[
            VMEM((2 * half, near.shape[1]), jnp.bfloat16),
            VMEM((2 * half, weight_out[0].shape[0]), jnp.bfloat16),
        ],
        compiler_params=pltpu.CompilerParams(vmem_limit_bytes=20 << 20),
        cost_estimate=pl.CostEstimate(
            flops=6 * half * pair * weight_in[0].size, bytes_accessed=8 << 20, transcendentals=0
        ),
    )(*hold(near, far, *weight_in, *weight_out))


def join(operands, *after):
    count = len(operands)

    def kernel(*refs):
        refs[-1][...] = jnp.concatenate([r[...] for r in refs[:count]], axis=0)

    shape = (sum(a.shape[0] for a in operands), operands[0].shape[1])
    return local_call(kernel, [shape], [*operands, *after])[0]


def fold_kernel(near, far, *outs):
    total = near[...].astype(jnp.float32) + far[...].astype(jnp.float32)
    at = 0
    for out in outs:
        out[...] = total[at : at + out.shape[0]].astype(jnp.bfloat16)
        at += out.shape[0]


def split_kernel(count, rows, head, head_got, *refs):
    top = head[...].astype(jnp.float32) + head_got[...].astype(jnp.float32)
    low = sum(r[...].astype(jnp.float32) for r in refs[:count])
    both = jnp.concatenate([top, low], axis=0)
    for i, out in enumerate(refs[count:]):
        out[...] = both[i * rows : (i + 1) * rows].astype(jnp.bfloat16)


def shards(tokens, node_list, gates, row_source, expert_in, expert_out):
    rows, width = tokens.shape
    nodes = lax.axis_size("node")
    locals_ = lax.axis_size("local")
    count = nodes * locals_
    step = 2 * locals_
    across = range(1, nodes // 2)
    beyond = range(2, locals_)
    message = pack(tokens, gates, node_list, row_source)
    weights, early = zip(*sort_weights(expert_in, expert_out))
    tail = [swap(message, k, count) for k in beyond]
    head = [message] + [swap(message, a * step, count) for a in across]
    head, tail = join(head, early[0]), join(tail, early[0])
    near = [head, tail, swap(head, 1, count)] + [swap(tail, a * step, count) for a in across]
    near = join(near, *early[1:])
    late = load(expert_out, sum(a.shape[1] for a in early), near)
    near_out, far_out = experts(
        gates.shape[1], rows, near, swap(near, locals_, count), weights, (*early, late)
    )
    sizes = [head.shape[0], tail.shape[0], head.shape[0]] + [tail.shape[0]] * len(across)
    head, tail, side, *sides = local_call(
        fold_kernel, [(s, width) for s in sizes], [near_out, swap(far_out, locals_, count)]
    )
    head_got = swap(side, 1, count)
    tail_got = [swap(v, a * step, count) for a, v in zip(across, sides)]
    own, *others = local_call(
        functools.partial(split_kernel, 1 + len(across), rows),
        [(rows, width)] * (1 + len(across) + len(beyond)),
        [head, head_got, tail, *tail_got],
    )
    masks = [a * step for a in across] + list(beyond)
    got = [swap(v, m, count) for m, v in reversed(list(zip(masks, others)))]
    return sum(v.astype(jnp.float32) for v in [own, *got]).astype(jnp.bfloat16)


def solution(mesh):
    spec = P(("groups", "node", "local"), None)
    return jax.shard_map(
        shards,
        mesh=mesh,
        in_specs=(spec, spec, spec, spec, P("node", None, None, "local"), P("node", "local", None)),
        out_specs=spec,
        check_vma=False,
    )
```

```python
import functools

import jax
import jax.numpy as jnp
from jax import lax
from jax.experimental import pallas as pl
from jax.experimental.pallas import tpu as pltpu
from jax.sharding import PartitionSpec as P

AXES = ("node", "local")
VMEM = pltpu.VMEM
LANES = 128
BUFFERS = 8
PIECE = 1024
EARLY = (2, 2)
SMALL = pltpu.CompilerParams(vmem_limit_bytes=4 << 20)


def swap(value, mask, count):
    return lax.ppermute(value, AXES, [(i, i ^ mask) for i in range(count)])


def in_vmem(count):
    return [pl.BlockSpec(memory_space=VMEM)] * count


def hold(*arrays):
    return [pltpu.with_memory_space_constraint(a, VMEM) for a in arrays]


def local_call(kernel, shapes, operands):
    return pl.pallas_call(
        kernel,
        out_shape=tuple(VMEM(s, jnp.bfloat16) for s in shapes),
        in_specs=in_vmem(len(operands)),
        out_specs=tuple(in_vmem(len(shapes))),
        compiler_params=SMALL,
    )(*hold(*operands))


def pack_kernel(tokens, gates, nodes, source, out):
    rows, width = tokens.shape
    chosen = gates.shape[1]
    slots = nodes.shape[0]
    out[:, :width] = tokens[...]
    tail = jnp.concatenate(
        [gates[...].astype(jnp.float32), jnp.zeros((rows, LANES - chosen), jnp.float32)], axis=1
    )
    row = lax.broadcasted_iota(jnp.int32, (rows, LANES), 0)
    lane = lax.broadcasted_iota(jnp.int32, (rows, LANES), 1)
    for r in range(rows):
        numbers = [nodes[j, r] for j in range(slots)] + [source[0, r]]
        for j, number in enumerate(numbers):
            tail = jnp.where((row == r) & (lane == chosen + j), number.astype(jnp.float32), tail)
    out[:, width:] = tail.astype(jnp.bfloat16)


def pack(tokens, gates, node_list, row_source):
    rows, width = tokens.shape
    return pl.pallas_call(
        pack_kernel,
        out_shape=VMEM((rows, width + LANES), jnp.bfloat16),
        in_specs=in_vmem(2) + [pl.BlockSpec(memory_space=pltpu.SMEM)] * 2,
        out_specs=pl.BlockSpec(memory_space=VMEM),
    )(tokens, gates, node_list.T, row_source)


def sort_kernel(chunk, kinds, expert, start_at, source, down, out, part, buffer, wide, sem, down_sem):
    _, total, _ = source.shape
    count = total // chunk
    depth = chunk // kinds

    def fetch(i, slot):
        start = pl.multiple_of(i * chunk, chunk)
        return pltpu.make_async_copy(
            source.at[expert, pl.ds(start, chunk)], buffer.at[slot], sem.at[slot]
        )

    for i in range(BUFFERS - 1):
        fetch(i, i).start()
    extra = pltpu.make_async_copy(down.at[:, pl.ds(start_at, part.shape[1])], part, down_sem)
    extra.start()

    @pl.loop(0, count)
    def _(i):
        slot = lax.rem(i, BUFFERS)

        @pl.when(i + BUFFERS - 1 < count)
        def _():
            fetch(i + BUFFERS - 1, lax.rem(i + BUFFERS - 1, BUFFERS)).start()

        fetch(i, slot).wait()
        wide[...] = buffer[slot].astype(jnp.float32)
        at = pl.multiple_of(i * depth, depth)
        for k in range(kinds):
            column = (k % 2) * (kinds // 2) + k // 2
            out[pl.ds(at, depth), column * LANES : (column + 1) * LANES] = wide[
                pl.ds(k, depth, stride=kinds), :
            ].astype(jnp.bfloat16)

    extra.wait()


def sort_weights(weight, down):
    pair, depth, two, units = weight.shape
    blocks = units // LANES
    kinds = two * blocks
    view = (
        weight.reshape(pair, depth, two, blocks, LANES)
        .transpose(0, 1, 3, 2, 4)
        .reshape(pair, depth * kinds, LANES)
    )
    chunk = 512 * kinds
    down = down.reshape(-1, depth)
    ends = [sum(EARLY[:e]) * PIECE for e in range(pair + 1)]
    source = [pltpu.with_memory_space_constraint(a, pltpu.HBM) for a in (view, down)]
    return [
        pl.pallas_call(
            functools.partial(sort_kernel, chunk, kinds, expert, ends[expert]),
            out_shape=(
                VMEM((depth, two * units), jnp.bfloat16),
                VMEM((down.shape[0], ends[expert + 1] - ends[expert]), jnp.bfloat16),
            ),
            in_specs=[pl.BlockSpec(memory_space=pltpu.HBM)] * 2,
            out_specs=tuple(in_vmem(2)),
            scratch_shapes=[
                VMEM((BUFFERS, chunk, LANES), jnp.bfloat16),
                VMEM((chunk, LANES), jnp.float32),
                pltpu.SemaphoreType.DMA((BUFFERS,)),
                pltpu.SemaphoreType.DMA,
            ],
            compiler_params=pltpu.CompilerParams(vmem_limit_bytes=8 << 20),
            cost_estimate=pl.CostEstimate(
                flops=0, bytes_accessed=2 * weight.size, transcendentals=0
            ),
        )(*source)
        for expert in range(pair)
    ]


def expert_kernel(chosen, pair, rows, near, far, *refs):
    weight_in, weight_out = refs[:pair], refs[pair:-4]
    near_out, far_out, held, hidden = refs[-4:]
    half = near.shape[0]
    depth, columns = weight_in[0].shape
    units = columns // 2
    slots = chosen // pair
    total = 2 * half
    held[:half] = near[...]
    held[half:] = far[...]
    tail = held[:, depth:].astype(jnp.float32)
    node = lax.axis_index("node").astype(jnp.float32)
    active = []
    for e in range(pair):
        gate = jnp.zeros((total, 1), jnp.float32)
        for j in range(slots):
            listed = tail[:, chosen + j : chosen + j + 1] == node
            gate = gate + jnp.where(listed, tail[:, pair * j + e : pair * j + e + 1], 0.0)
        first = jnp.dot(held[:, :depth], weight_in[e][:, :units], preferred_element_type=jnp.float32)
        second = jnp.dot(
            held[:, :depth], weight_in[e][:, units:], preferred_element_type=jnp.float32
        )
        active.append((first / (1.0 + jnp.exp(-first)) * second * gate).astype(jnp.bfloat16))
    row = lax.broadcasted_iota(jnp.int32, (total, total), 0)
    column = lax.broadcasted_iota(jnp.int32, (total, total), 1)
    source = tail[:, chosen + slots : chosen + slots + 1].astype(jnp.int32)
    order = (column == row - lax.rem(row, rows) + source).astype(jnp.bfloat16)
    hidden[...] = jnp.dot(
        order, jnp.concatenate(active, axis=1), preferred_element_type=jnp.float32
    ).astype(jnp.bfloat16)
    at = 0
    for down in weight_out:
        for i in range(down.shape[1] // PIECE):
            result = jnp.dot(
                hidden[...],
                down[:, i * PIECE : (i + 1) * PIECE],
                preferred_element_type=jnp.float32,
            ).astype(jnp.bfloat16)
            near_out[:, at : at + PIECE] = result[:half]
            far_out[:, at : at + PIECE] = result[half:]
            at += PIECE


def load_kernel(begin, source, after, out, sem):
    copy = pltpu.make_async_copy(source.at[:, pl.ds(begin, out.shape[1])], out, sem)
    copy.start()
    copy.wait()


def load(weight_out, begin, after):
    weight_out = pltpu.with_memory_space_constraint(
        weight_out.reshape(-1, weight_out.shape[-1]), pltpu.HBM
    )
    height, depth = weight_out.shape
    return pl.pallas_call(
        functools.partial(load_kernel, begin),
        out_shape=VMEM((height, depth - begin), jnp.bfloat16),
        in_specs=[pl.BlockSpec(memory_space=pltpu.HBM)] + in_vmem(1),
        out_specs=pl.BlockSpec(memory_space=VMEM),
        scratch_shapes=[pltpu.SemaphoreType.DMA],
        compiler_params=SMALL,
        cost_estimate=pl.CostEstimate(
            flops=0, bytes_accessed=2 * height * (depth - begin), transcendentals=0
        ),
    )(weight_out, *hold(after))


def experts(chosen, rows, near, far, weight_in, weight_out):
    half = near.shape[0]
    pair = len(weight_in)
    depth, columns = weight_in[0].shape
    return pl.pallas_call(
        functools.partial(expert_kernel, chosen, pair, rows),
        out_shape=(VMEM((half, depth), jnp.bfloat16),) * 2,
        in_specs=in_vmem(2 + pair + len(weight_out)),
        out_specs=tuple(in_vmem(2)),
        scratch_shapes=[
            VMEM((2 * half, near.shape[1]), jnp.bfloat16),
            VMEM((2 * half, weight_out[0].shape[0]), jnp.bfloat16),
        ],
        compiler_params=pltpu.CompilerParams(vmem_limit_bytes=20 << 20),
        cost_estimate=pl.CostEstimate(
            flops=6 * half * pair * weight_in[0].size, bytes_accessed=8 << 20, transcendentals=0
        ),
    )(*hold(near, far, *weight_in, *weight_out))


def join(operands, *after):
    count = len(operands)

    def kernel(*refs):
        refs[-1][...] = jnp.concatenate([r[...] for r in refs[:count]], axis=0)

    shape = (sum(a.shape[0] for a in operands), operands[0].shape[1])
    return local_call(kernel, [shape], [*operands, *after])[0]


def fold_kernel(rows, groups, near, far, *refs):
    total = near[...].astype(jnp.float32) + far[...].astype(jnp.float32)
    for group, out in zip(groups, refs[len(refs) - len(groups) :]):
        pieces = [total[i * rows : (i + 1) * rows] for i in group]
        out[...] = jnp.concatenate(pieces, axis=0).astype(jnp.bfloat16)


def split_kernel(count, rows, *refs):
    total = sum(r[...].astype(jnp.float32) for r in refs[:count])
    for i, out in enumerate(refs[count:]):
        out[...] = total[i * rows : (i + 1) * rows].astype(jnp.bfloat16)


def shards(tokens, node_list, gates, row_source, expert_in, expert_out):
    rows, width = tokens.shape
    nodes = lax.axis_size("node")
    locals_ = lax.axis_size("local")
    count = nodes * locals_
    step = 2 * locals_
    across = range(1, nodes // 2)
    beyond = range(2, locals_)
    message = pack(tokens, gates, node_list, row_source)
    weights, early = zip(*sort_weights(expert_in, expert_out))
    tail = [swap(message, k, count) for k in beyond]
    head = [message] + [swap(message, a * step, count) for a in across]
    head, tail = join(head, early[0]), join(tail, early[0])
    near = [head, tail, swap(head, 1, count)] + [swap(tail, a * step, count) for a in across]
    near = join(near, *early[1:])
    late = load(expert_out, sum(a.shape[1] for a in early), near)
    near_out, far_out = experts(
        gates.shape[1], rows, near, swap(near, locals_, count), weights, (*early, late)
    )
    everywhere = [0, *across]
    places = [(a, 0) for a in everywhere] + [(0, b) for b in beyond]
    places += [(a, 1) for a in everywhere] + [(a, b) for a in across for b in beyond]
    index = {place: i for i, place in enumerate(places)}
    far_got = swap(far_out, locals_, count)
    merged = [0, *range(2, locals_, 2)]

    def fold(groups, *after):
        return local_call(
            functools.partial(fold_kernel, rows, [[index[p] for p in g] for g in groups]),
            [(len(g) * rows, width) for g in groups],
            [near_out, far_got, *after],
        )

    def send(blocks, after):
        arrays = fold([[p] for p in blocks], after)
        return [swap(v, a * step + b, count) for v, (a, b) in zip(arrays, blocks)], arrays[0]

    kept, *crossing = fold([[(a, b) for b in merged] for a in everywhere])
    crossed = [swap(v, a * step, count) for a, v in zip(across, crossing)]
    middle, done = [], kept
    for b in range(3, locals_, 2):
        for a in reversed(everywhere):
            sent, done = send([(a, b)], done)
            middle += sent
    beside, _ = send([(a, 1) for a in everywhere], done)
    own, *last = local_call(
        functools.partial(split_kernel, 1 + len(crossed), rows),
        [(rows, width)] * len(merged),
        [kept, *crossed],
    )
    last = [swap(v, b, count) for v, b in zip(last, merged[1:])]
    return sum(v.astype(jnp.float32) for v in [own, *middle, *beside, *last]).astype(jnp.bfloat16)


def solution(mesh):
    spec = P(("groups", "node", "local"), None)
    return jax.shard_map(
        shards,
        mesh=mesh,
        in_specs=(spec, spec, spec, spec, P("node", None, None, "local"), P("node", "local", None)),
        out_specs=spec,
        check_vma=False,
    )
```

```python
import functools

import jax
import jax.numpy as jnp
from jax import lax
from jax.experimental import pallas as pl
from jax.experimental.pallas import tpu as pltpu
from jax.sharding import PartitionSpec as P

AXES = ("node", "local")
VMEM = pltpu.VMEM
LANES = 128
BUFFERS = 8
SMALL = pltpu.CompilerParams(vmem_limit_bytes=4 << 20)


def swap(value, mask, count):
    return lax.ppermute(value, AXES, [(i, i ^ mask) for i in range(count)])


def in_vmem(count):
    return [pl.BlockSpec(memory_space=VMEM)] * count


def hold(*arrays):
    return [pltpu.with_memory_space_constraint(a, VMEM) for a in arrays]


def local_call(kernel, shapes, operands):
    return pl.pallas_call(
        kernel,
        out_shape=tuple(VMEM(s, jnp.bfloat16) for s in shapes),
        in_specs=in_vmem(len(operands)),
        out_specs=tuple(in_vmem(len(shapes))),
        compiler_params=SMALL,
    )(*hold(*operands))


def pack_kernel(tokens, gates, nodes, source, out):
    rows, width = tokens.shape
    chosen = gates.shape[1]
    slots = nodes.shape[0]
    out[:, :width] = tokens[...]
    tail = jnp.concatenate(
        [gates[...].astype(jnp.float32), jnp.zeros((rows, LANES - chosen), jnp.float32)], axis=1
    )
    row = lax.broadcasted_iota(jnp.int32, (rows, LANES), 0)
    lane = lax.broadcasted_iota(jnp.int32, (rows, LANES), 1)
    for r in range(rows):
        numbers = [nodes[j, r] for j in range(slots)] + [source[0, r]]
        for j, number in enumerate(numbers):
            tail = jnp.where((row == r) & (lane == chosen + j), number.astype(jnp.float32), tail)
    out[:, width:] = tail.astype(jnp.bfloat16)


def pack(tokens, gates, node_list, row_source):
    rows, width = tokens.shape
    return pl.pallas_call(
        pack_kernel,
        out_shape=VMEM((rows, width + LANES), jnp.bfloat16),
        in_specs=in_vmem(2) + [pl.BlockSpec(memory_space=pltpu.SMEM)] * 2,
        out_specs=pl.BlockSpec(memory_space=VMEM),
    )(tokens, gates, node_list.T, row_source)


def sort_kernel(chunk, kinds, expert, source, out, token, buffer, wide, sem):
    _, total, _ = source.shape
    count = total // chunk
    depth = chunk // kinds

    def fetch(i, slot):
        start = pl.multiple_of(i * chunk, chunk)
        return pltpu.make_async_copy(
            source.at[expert, pl.ds(start, chunk)], buffer.at[slot], sem.at[slot]
        )

    for i in range(BUFFERS - 1):
        fetch(i, i).start()

    @pl.loop(0, count)
    def _(i):
        slot = lax.rem(i, BUFFERS)

        @pl.when(i + BUFFERS - 1 < count)
        def _():
            fetch(i + BUFFERS - 1, lax.rem(i + BUFFERS - 1, BUFFERS)).start()

        fetch(i, slot).wait()
        wide[...] = buffer[slot].astype(jnp.float32)
        at = pl.multiple_of(i * depth, depth)
        for k in range(kinds):
            column = (k % 2) * (kinds // 2) + k // 2
            out[pl.ds(at, depth), column * LANES : (column + 1) * LANES] = wide[
                pl.ds(k, depth, stride=kinds), :
            ].astype(jnp.bfloat16)

    token[...] = jnp.zeros_like(token)


def sort_weights(weight):
    pair, depth, two, units = weight.shape
    blocks = units // LANES
    kinds = two * blocks
    view = (
        weight.reshape(pair, depth, two, blocks, LANES)
        .transpose(0, 1, 3, 2, 4)
        .reshape(pair, depth * kinds, LANES)
    )
    chunk = 512 * kinds
    view = pltpu.with_memory_space_constraint(view, pltpu.HBM)
    return [
        pl.pallas_call(
            functools.partial(sort_kernel, chunk, kinds, expert),
            out_shape=(
                VMEM((depth, two * units), jnp.bfloat16),
                VMEM((16, LANES), jnp.bfloat16),
            ),
            in_specs=[pl.BlockSpec(memory_space=pltpu.HBM)],
            out_specs=tuple(in_vmem(2)),
            scratch_shapes=[
                VMEM((BUFFERS, chunk, LANES), jnp.bfloat16),
                VMEM((chunk, LANES), jnp.float32),
                pltpu.SemaphoreType.DMA((BUFFERS,)),
            ],
            compiler_params=pltpu.CompilerParams(vmem_limit_bytes=8 << 20),
            cost_estimate=pl.CostEstimate(
                flops=0, bytes_accessed=2 * weight.size, transcendentals=0
            ),
        )(view)
        for expert in range(pair)
    ]


def expert_kernel(chosen, pair, rows, near, far, *refs):
    weight_in = refs[:pair]
    hidden, held = refs[pair:]
    half = near.shape[0]
    depth, columns = weight_in[0].shape
    units = columns // 2
    slots = chosen // pair
    total = 2 * half
    held[:half] = near[...]
    held[half:] = far[...]
    tail = held[:, depth:].astype(jnp.float32)
    node = lax.axis_index("node").astype(jnp.float32)
    active = []
    for e in range(pair):
        gate = jnp.zeros((total, 1), jnp.float32)
        for j in range(slots):
            listed = tail[:, chosen + j : chosen + j + 1] == node
            gate = gate + jnp.where(listed, tail[:, pair * j + e : pair * j + e + 1], 0.0)
        first = jnp.dot(held[:, :depth], weight_in[e][:, :units], preferred_element_type=jnp.float32)
        second = jnp.dot(
            held[:, :depth], weight_in[e][:, units:], preferred_element_type=jnp.float32
        )
        active.append((first / (1.0 + jnp.exp(-first)) * second * gate).astype(jnp.bfloat16))
    row = lax.broadcasted_iota(jnp.int32, (total, total), 0)
    column = lax.broadcasted_iota(jnp.int32, (total, total), 1)
    source = tail[:, chosen + slots : chosen + slots + 1].astype(jnp.int32)
    order = (column == row - lax.rem(row, rows) + source).astype(jnp.bfloat16)
    hidden[...] = jnp.dot(
        order, jnp.concatenate(active, axis=1), preferred_element_type=jnp.float32
    ).astype(jnp.bfloat16)


def experts(chosen, rows, near, far, weight_in):
    half = near.shape[0]
    pair = len(weight_in)
    depth, columns = weight_in[0].shape
    return pl.pallas_call(
        functools.partial(expert_kernel, chosen, pair, rows),
        out_shape=VMEM((2 * half, pair * columns // 2), jnp.bfloat16),
        in_specs=in_vmem(2 + pair),
        out_specs=pl.BlockSpec(memory_space=VMEM),
        scratch_shapes=[
            VMEM((2 * half, near.shape[1]), jnp.bfloat16),
        ],
        compiler_params=pltpu.CompilerParams(vmem_limit_bytes=20 << 20),
        cost_estimate=pl.CostEstimate(
            flops=6 * half * pair * weight_in[0].size, bytes_accessed=8 << 20, transcendentals=0
        ),
    )(*hold(near, far, *weight_in))


def join(operands, *after):
    count = len(operands)

    def kernel(*refs):
        refs[-1][...] = jnp.concatenate([r[...] for r in refs[:count]], axis=0)

    shape = (sum(a.shape[0] for a in operands), operands[0].shape[1])
    return local_call(kernel, [shape], [*operands, *after])[0]


def fold_kernel(rows, groups, near, far, *refs):
    total = near[...].astype(jnp.float32) + far[...].astype(jnp.float32)
    for group, out in zip(groups, refs[len(refs) - len(groups) :]):
        pieces = [total[i * rows : (i + 1) * rows] for i in group]
        out[...] = jnp.concatenate(pieces, axis=0).astype(jnp.bfloat16)


def split_kernel(count, rows, *refs):
    total = sum(r[...].astype(jnp.float32) for r in refs[:count])
    for i, out in enumerate(refs[count:]):
        out[...] = total[i * rows : (i + 1) * rows].astype(jnp.bfloat16)


def shards(tokens, node_list, gates, row_source, expert_in, expert_out):
    rows, width = tokens.shape
    nodes = lax.axis_size("node")
    locals_ = lax.axis_size("local")
    count = nodes * locals_
    step = 2 * locals_
    across = range(1, nodes // 2)
    beyond = range(2, locals_)
    message = pack(tokens, gates, node_list, row_source)
    weights, early = zip(*sort_weights(expert_in))
    tail = [swap(message, k, count) for k in beyond]
    head = [message] + [swap(message, a * step, count) for a in across]
    head, tail = join(head, early[0]), join(tail, early[0])
    near = [head, tail, swap(head, 1, count)] + [swap(tail, a * step, count) for a in across]
    near = join(near, *early[1:])
    hidden = experts(gates.shape[1], rows, near, swap(near, locals_, count), weights)
    down = expert_out.reshape(-1, width)
    half = near.shape[0]
    out = jnp.dot(hidden, down, preferred_element_type=jnp.float32).astype(jnp.bfloat16)
    near_out, far_out = out[:half], out[half:]
    everywhere = [0, *across]
    places = [(a, 0) for a in everywhere] + [(0, b) for b in beyond]
    places += [(a, 1) for a in everywhere] + [(a, b) for a in across for b in beyond]
    index = {place: i for i, place in enumerate(places)}
    far_got = swap(far_out, locals_, count)
    merged = [0, *range(2, locals_, 2)]

    def fold(groups, *after):
        return local_call(
            functools.partial(fold_kernel, rows, [[index[p] for p in g] for g in groups]),
            [(len(g) * rows, width) for g in groups],
            [near_out, far_got, *after],
        )

    def send(blocks, after):
        arrays = fold([[p] for p in blocks], after)
        return [swap(v, a * step + b, count) for v, (a, b) in zip(arrays, blocks)], arrays[0]

    kept, *crossing = fold([[(a, b) for b in merged] for a in everywhere])
    crossed = [swap(v, a * step, count) for a, v in zip(across, crossing)]
    middle, done = [], kept
    for b in range(3, locals_, 2):
        for a in reversed(everywhere):
            sent, done = send([(a, b)], done)
            middle += sent
    beside, _ = send([(a, 1) for a in reversed(everywhere)], done)
    own, *last = local_call(
        functools.partial(split_kernel, 1 + len(crossed), rows),
        [(rows, width)] * len(merged),
        [kept, *crossed],
    )
    last = [swap(v, b, count) for v, b in zip(last, merged[1:])]
    return sum(v.astype(jnp.float32) for v in [own, *middle, *beside, *last]).astype(jnp.bfloat16)


def solution(mesh):
    spec = P(("groups", "node", "local"), None)
    return jax.shard_map(
        shards,
        mesh=mesh,
        in_specs=(spec, spec, spec, spec, P("node", None, None, "local"), P("node", "local", None)),
        out_specs=spec,
        check_vma=False,
    )
```

```python
import functools

import jax
import jax.numpy as jnp
from jax import lax
from jax.experimental import pallas as pl
from jax.experimental.pallas import tpu as pltpu
from jax.sharding import PartitionSpec as P

AXES = ("node", "local")
VMEM = pltpu.VMEM
LANES = 128
BUFFERS = 8
SMALL = pltpu.CompilerParams(vmem_limit_bytes=4 << 20)


def swap(value, mask, count):
    return lax.ppermute(value, AXES, [(i, i ^ mask) for i in range(count)])


def in_vmem(count):
    return [pl.BlockSpec(memory_space=VMEM)] * count


def hold(*arrays):
    return [pltpu.with_memory_space_constraint(a, VMEM) for a in arrays]


def local_call(kernel, shapes, operands):
    return pl.pallas_call(
        kernel,
        out_shape=tuple(VMEM(s, jnp.bfloat16) for s in shapes),
        in_specs=in_vmem(len(operands)),
        out_specs=tuple(in_vmem(len(shapes))),
        compiler_params=SMALL,
    )(*hold(*operands))


def pack_kernel(tokens, gates, nodes, source, out):
    rows, width = tokens.shape
    chosen = gates.shape[1]
    slots = nodes.shape[0]
    out[:, :width] = tokens[...]
    tail = jnp.concatenate(
        [gates[...].astype(jnp.float32), jnp.zeros((rows, LANES - chosen), jnp.float32)], axis=1
    )
    row = lax.broadcasted_iota(jnp.int32, (rows, LANES), 0)
    lane = lax.broadcasted_iota(jnp.int32, (rows, LANES), 1)
    for r in range(rows):
        numbers = [nodes[j, r] for j in range(slots)] + [source[0, r]]
        for j, number in enumerate(numbers):
            tail = jnp.where((row == r) & (lane == chosen + j), number.astype(jnp.float32), tail)
    out[:, width:] = tail.astype(jnp.bfloat16)


def pack(tokens, gates, node_list, row_source):
    rows, width = tokens.shape
    return pl.pallas_call(
        pack_kernel,
        out_shape=VMEM((rows, width + LANES), jnp.bfloat16),
        in_specs=in_vmem(2) + [pl.BlockSpec(memory_space=pltpu.SMEM)] * 2,
        out_specs=pl.BlockSpec(memory_space=VMEM),
    )(tokens, gates, node_list.T, row_source)


def sort_kernel(chunk, kinds, expert, source, out, token, buffer, wide, sem):
    _, total, _ = source.shape
    count = total // chunk
    depth = chunk // kinds

    def fetch(i, slot):
        start = pl.multiple_of(i * chunk, chunk)
        return pltpu.make_async_copy(
            source.at[expert, pl.ds(start, chunk)], buffer.at[slot], sem.at[slot]
        )

    for i in range(BUFFERS - 1):
        fetch(i, i).start()

    @pl.loop(0, count)
    def _(i):
        slot = lax.rem(i, BUFFERS)

        @pl.when(i + BUFFERS - 1 < count)
        def _():
            fetch(i + BUFFERS - 1, lax.rem(i + BUFFERS - 1, BUFFERS)).start()

        fetch(i, slot).wait()
        wide[...] = buffer[slot].astype(jnp.float32)
        at = pl.multiple_of(i * depth, depth)
        for k in range(kinds):
            column = (k % 2) * (kinds // 2) + k // 2
            out[pl.ds(at, depth), column * LANES : (column + 1) * LANES] = wide[
                pl.ds(k, depth, stride=kinds), :
            ].astype(jnp.bfloat16)

    token[...] = jnp.zeros_like(token)


def sort_weights(weight):
    pair, depth, two, units = weight.shape
    blocks = units // LANES
    kinds = two * blocks
    view = (
        weight.reshape(pair, depth, two, blocks, LANES)
        .transpose(0, 1, 3, 2, 4)
        .reshape(pair, depth * kinds, LANES)
    )
    chunk = 512 * kinds
    view = pltpu.with_memory_space_constraint(view, pltpu.HBM)
    return [
        pl.pallas_call(
            functools.partial(sort_kernel, chunk, kinds, expert),
            out_shape=(
                VMEM((depth, two * units), jnp.bfloat16),
                VMEM((16, LANES), jnp.bfloat16),
            ),
            in_specs=[pl.BlockSpec(memory_space=pltpu.HBM)],
            out_specs=tuple(in_vmem(2)),
            scratch_shapes=[
                VMEM((BUFFERS, chunk, LANES), jnp.bfloat16),
                VMEM((chunk, LANES), jnp.float32),
                pltpu.SemaphoreType.DMA((BUFFERS,)),
            ],
            compiler_params=pltpu.CompilerParams(vmem_limit_bytes=8 << 20),
            cost_estimate=pl.CostEstimate(
                flops=0, bytes_accessed=2 * weight.size, transcendentals=0
            ),
        )(view)
        for expert in range(pair)
    ]


def expert_kernel(chosen, pair, rows, blocks, *refs):
    weight_in = refs[blocks:-2]
    hidden, held = refs[-2:]
    total = held.shape[0]
    depth, columns = weight_in[0].shape
    units = columns // 2
    slots = chosen // pair
    at = 0
    for block in refs[:blocks]:
        held[at : at + block.shape[0]] = block[...]
        at += block.shape[0]
    tail = held[:, depth:].astype(jnp.float32)
    node = lax.axis_index("node").astype(jnp.float32)
    active = []
    for e in range(pair):
        gate = jnp.zeros((total, 1), jnp.float32)
        for j in range(slots):
            listed = tail[:, chosen + j : chosen + j + 1] == node
            gate = gate + jnp.where(listed, tail[:, pair * j + e : pair * j + e + 1], 0.0)
        first = jnp.dot(held[:, :depth], weight_in[e][:, :units], preferred_element_type=jnp.float32)
        second = jnp.dot(
            held[:, :depth], weight_in[e][:, units:], preferred_element_type=jnp.float32
        )
        active.append((first / (1.0 + jnp.exp(-first)) * second * gate).astype(jnp.bfloat16))
    row = lax.broadcasted_iota(jnp.int32, (total, total), 0)
    column = lax.broadcasted_iota(jnp.int32, (total, total), 1)
    source = tail[:, chosen + slots : chosen + slots + 1].astype(jnp.int32)
    order = (column == row - lax.rem(row, rows) + source).astype(jnp.bfloat16)
    hidden[...] = jnp.dot(
        order, jnp.concatenate(active, axis=1), preferred_element_type=jnp.float32
    ).astype(jnp.bfloat16)


def experts(chosen, rows, blocks, weight_in):
    total = sum(a.shape[0] for a in blocks)
    pair = len(weight_in)
    columns = weight_in[0].shape[1]
    return pl.pallas_call(
        functools.partial(expert_kernel, chosen, pair, rows, len(blocks)),
        out_shape=VMEM((total, pair * columns // 2), jnp.bfloat16),
        in_specs=in_vmem(len(blocks) + pair),
        out_specs=pl.BlockSpec(memory_space=VMEM),
        scratch_shapes=[VMEM((total, blocks[0].shape[1]), jnp.bfloat16)],
        compiler_params=pltpu.CompilerParams(vmem_limit_bytes=20 << 20),
        cost_estimate=pl.CostEstimate(
            flops=3 * total * pair * weight_in[0].size, bytes_accessed=8 << 20, transcendentals=0
        ),
    )(*hold(*blocks, *weight_in))


def join(operands, *after):
    count = len(operands)

    def kernel(*refs):
        refs[-1][...] = jnp.concatenate([r[...] for r in refs[:count]], axis=0)

    shape = (sum(a.shape[0] for a in operands), operands[0].shape[1])
    return local_call(kernel, [shape], [*operands, *after])[0]


def fold_kernel(rows, groups, near, far, *refs):
    total = near[...].astype(jnp.float32) + far[...].astype(jnp.float32)
    for group, out in zip(groups, refs[len(refs) - len(groups) :]):
        pieces = [total[i * rows : (i + 1) * rows] for i in group]
        out[...] = jnp.concatenate(pieces, axis=0).astype(jnp.bfloat16)


def split_kernel(rows, tops, count, begin, kept, *refs):
    outs = refs[len(refs) - tops :] if tops else refs[count:]
    size = len(outs) * rows
    total = kept[...].astype(jnp.float32)[begin : begin + size]
    total += sum(r[...].astype(jnp.float32) for r in refs[:count])
    for i, out in enumerate(outs):
        out[...] = total[i * rows : (i + 1) * rows].astype(jnp.bfloat16)


def shards(tokens, node_list, gates, row_source, expert_in, expert_out):
    rows, width = tokens.shape
    nodes = lax.axis_size("node")
    locals_ = lax.axis_size("local")
    count = nodes * locals_
    step = 2 * locals_
    across = range(1, nodes // 2)
    beyond = range(2, locals_)
    message = pack(tokens, gates, node_list, row_source)
    weights, early = zip(*sort_weights(expert_in))
    tail = [swap(message, k, count) for k in beyond]
    head = [message] + [swap(message, a * step, count) for a in across]
    head, tail = join(head, early[0]), join(tail, early[0])
    near = join([head, tail])
    far = swap(near, locals_, count)
    side = [swap(head, 1, count)] + [swap(tail, a * step, count) for a in across]
    side = join(side, *early[1:])
    hidden = experts(gates.shape[1], rows, [near, side, far, swap(side, locals_, count)], weights)
    down = expert_out.reshape(-1, width)
    half = hidden.shape[0] // 2
    out = jnp.dot(hidden, down, preferred_element_type=jnp.float32).astype(jnp.bfloat16)
    near_out, far_out = out[:half], out[half:]
    everywhere = [0, *across]
    places = [(a, 0) for a in everywhere] + [(0, b) for b in beyond]
    places += [(a, 1) for a in everywhere] + [(a, b) for a in across for b in beyond]
    index = {place: i for i, place in enumerate(places)}
    far_got = swap(far_out, locals_, count)
    even = range(2, locals_, 2)

    def fold(groups, *after):
        return local_call(
            functools.partial(fold_kernel, rows, [[index[p] for p in g] for g in groups]),
            [(len(g) * rows, width) for g in groups],
            [near_out, far_got, *after],
        )

    def send(blocks, after):
        arrays = fold([[p] for p in blocks], after)
        return [swap(v, a * step + b, count) for v, (a, b) in zip(arrays, blocks)], arrays[0]

    tops = [(a, 0) for a in everywhere]
    lows = [(0, b) for b in even]
    kept, *crossing = fold(
        [tops + lows, *[[(a, b) for b in even] for a in across]]
    )
    crossed = [swap(v, a * step, count) for a, v in zip(across, crossing)]
    middle, done = [], kept
    for b in range(3, locals_, 2):
        for a in reversed(everywhere):
            sent, done = send([(a, b)], done)
            middle += sent
    side, = fold([[(a, 1) for a in everywhere]], done)
    side = swap(side, 1, count)
    low_parts = local_call(
        functools.partial(split_kernel, rows, 0, len(crossed), len(tops) * rows),
        [(rows, width)] * len(lows),
        [kept, *crossed],
    )
    own, *top_parts = local_call(
        functools.partial(split_kernel, rows, len(tops), 1, 0),
        [(rows, width)] * len(tops),
        [kept, side, low_parts[0]],
    )
    last = [swap(v, b, count) for v, (_, b) in zip(low_parts, lows)]
    last += [swap(v, a * step, count) for v, (a, _) in zip(top_parts, tops[1:])]
    return sum(v.astype(jnp.float32) for v in [own, *middle, *last]).astype(jnp.bfloat16)


def solution(mesh):
    spec = P(("groups", "node", "local"), None)
    return jax.shard_map(
        shards,
        mesh=mesh,
        in_specs=(spec, spec, spec, spec, P("node", None, None, "local"), P("node", "local", None)),
        out_specs=spec,
        check_vma=False,
    )
```
